32 devices in a mesh: attn: 4 (over x, core), ffn: 8 (over z, y).
Axes of the slice: x: 2, y: 2, z: 4, core: 2. Of those that a mesh axis runs over, the one named last changes fastest.
Arguments:
- queries: bfloat16 [256, 2, 64, 576], P(('attn', 'ffn')), may hold values from -9 to 9
- latent_cache: bfloat16 [256, 512, 576], P(('attn', 'ffn')), may hold values from -4 to 4
- fresh_latent: bfloat16 [256, 2, 576], P(('attn', 'ffn')), may hold values from -4 to 4
- lengths: int32 [256], P(('attn', 'ffn')), may hold values from 1 to 512, 65536 in all
- handoff: int32 [8, 8], P('ffn'), may hold values 0 or 1
- residual: bfloat16 [256, 2, 7168], P(('attn', 'ffn')), may hold values from -30 to 30
- value_up_matrix: bfloat16 [64, 512, 128], P('ffn'), may hold values from -0.5 to 0.5
- output_weight: bfloat16 [8192, 7168], P('ffn'), may hold values from -0.1875 to 0.1875
- norm_gain: float32 [7168], replicated, may hold values from 0.3 to 3
- router: bfloat16 [7168, 8], replicated, may hold values from -0.0625 to 0.0625
- expert_ids: int32 [256, 2, 2], P('attn'), may hold values from 0 to 7, all different within a row; in each aligned block of 128 rows (0 to 127, 128 to 255, ..., all dimensions but the last counted through in order) at most 64 rows name the same one
- gate_weight: bfloat16 [8, 7168, 2048], P('ffn', None, 'attn'), may hold values from -0.0625 to 0.0625
- up_weight: bfloat16 [8, 7168, 2048], P('ffn', None, 'attn'), may hold values from -0.0625 to 0.0625
- down_weight: bfloat16 [8, 2048, 7168], P('ffn', 'attn'), may hold values from -0.125 to 0.125
Outputs:
- attended: bfloat16 [256, 2, 7168], P(('attn', 'ffn'))
- expert_out: bfloat16 [256, 2, 7168], P(('attn', 'ffn'))
The draws below stay inside these ranges and needn't reach their ends.
Inputs may be any that keep to these rules, and one draw needn't show every extreme that they name: `expert_ids`: the 2 ids of a token differ. In each aligned block of 128 tokens (the requests of one index of attn, all new tokens of each, in order) no expert is chosen by more than 64 tokens, and some expert is chosen by exactly 64 in some block.
All inputs are finite; a program needn't handle non-finite values. No bound on the sum of `lengths` or of `handoff` on one device may be relied on, other than what follows from the above.
Results may differ from the reference program's by a relative error of at most 0.014.
Values may be sent and summed in bfloat16 or wider, within the bound.
No kernel may reach another device: no remote copies, remote signals or barrier semaphores. Data moves between devices by JAX's collectives and lax.ppermute only.
A program may use at most 128 MiB of HBM per device.

```python
import math
import jax
import jax.numpy as jnp
import numpy as np
from jax import lax

D = 7168
HEADS = 64
KV_RANK = 512
LATENT = 576
V_HEAD = 128
EXP_W = 2048
TOP = 2
STEPS = 2
LEN = 512
REQ_DEV = 8
EXPERTS = 8
REQS = 256
ROW_REQ = 64
CAP = 64
N_ATTN = 4
N_FFN = 8


def leading_rows(key):
    base_key = jax.random.fold_in(key, 4101)
    return jax.random.truncated_normal(base_key, -4.0, 4.0, (REQS, 2, LATENT), jnp.float32)


def draw_latent_cache(key, part):
    front_rows = leading_rows(key)
    later_key = jax.random.fold_in(key, 4102)
    later_rows = jax.random.truncated_normal(later_key, -4.0, 4.0, (REQS, LEN - 2, LATENT), jnp.float32)
    return jnp.concatenate([front_rows, later_rows], axis=1).astype(jnp.bfloat16)


def draw_queries(key, part):
    base_key = jax.random.fold_in(key, 4201)
    shape_full = (REQS, STEPS, HEADS, LATENT)
    value_rows = jax.random.truncated_normal(base_key, -4.0, 4.0, shape_full, jnp.float32)
    return value_rows.astype(jnp.bfloat16)


def draw_residual(key, part):
    base_key = jax.random.fold_in(key, 4301)
    log_ten = math.log(10.0)
    per_row_scale = jnp.exp(jax.random.uniform(jax.random.fold_in(base_key, 1), (REQS, STEPS, 1), jnp.float32, 0.0, log_ten))
    column_scale = jnp.exp(jax.random.uniform(jax.random.fold_in(base_key, 2), (1, 1, D), jnp.float32, 0.0, log_ten))
    random_part = jax.random.truncated_normal(jax.random.fold_in(base_key, 4), -3.0, 3.0, (REQS, STEPS, D), jnp.float32)
    return (random_part * per_row_scale * column_scale * 0.1).astype(jnp.bfloat16)


def set_ends(drawn, key, smallest, high):
    spot = [jax.random.randint(jax.random.fold_in(key, axis), (), 0, length) for axis, length in enumerate(drawn.shape)]
    main_axis = drawn.shape.index(max(drawn.shape))
    neighbour = spot[:main_axis] + [(spot[main_axis] + 1) % drawn.shape[main_axis]] + spot[main_axis + 1:]
    return drawn.at[tuple(spot)].set(smallest).at[tuple(neighbour)].set(high)


def block_levels(stream_key, dims, split, smallest, largest):
    gain, own = 1.0, jax.random.fold_in(stream_key, 6)
    for dim, shards_of in split:
        heights = jnp.exp(jax.random.uniform(jax.random.fold_in(own, dim), (shards_of,), jnp.float32, smallest / len(split), largest / len(split)))
        gain = gain * jnp.repeat(heights, dims[dim] // shards_of).reshape([-1 if axis == dim else 1 for axis in range(len(dims))])
    return gain


def profile(count, total, reach, slope):
    weights = [(1 << 20) // math.isqrt(rank ** slope) + 1 for rank in range(2, count + 1)]
    rest, holding = total - reach - (count - 1), [1] * (count - 1)
    while rest > 0:
        candidates = [i for i in range(count - 1) if holding[i] < reach]
        pool, left = sum([weights[i] for i in candidates]), rest
        for i in candidates:
            addition = min(reach - holding[i], max(1, left * weights[i] // pool), rest)
            holding[i] = holding[i] + addition
            rest = rest - addition
    return np.array([reach] + holding)


def ragged_sizes(key, count, total, bound, lean):
    if count == 2:
        one = jax.random.randint(key, (), max(1, total - bound), min(bound, total - 1) + 1)
        return jnp.stack([one, total - one])
    sizes = jnp.asarray(profile(count, total, bound, lean), jnp.int32)
    pairs = (count - 1) // 2
    source_of, taker = sizes[1:1 + 2 * pairs:2], sizes[2:2 + 2 * pairs:2]
    slack = jnp.minimum(source_of - 1, bound - taker)
    passed = jax.random.randint(jax.random.fold_in(key, 1), (pairs,), 0, 1 << 20) % (slack + 1)
    sizes = sizes.at[1:1 + 2 * pairs:2].set(source_of - passed).at[2:2 + 2 * pairs:2].set(taker + passed)
    return sizes[jax.random.permutation(jax.random.fold_in(key, 2), count)]


def routed_block(rng, own, number, rows, count, top, reach, skew):
    sequence = jax.random.permutation(rng, count)
    crowded, usual = load_shares(count, rows * top, reach, skew, True), load_shares(count, rows * top, reach, skew, False)
    places = jnp.arange(count)

    def named(sizes, offset_by):
        used = int((sizes > 0).sum())
        fixed = max(1, used // 4)
        shifted = fixed + (places - fixed + offset_by * (used - fixed)) % max(1, count - fixed)
        return jnp.zeros((count,), jnp.int32).at[sequence[jnp.where(places < fixed, places, shifted)]].set(jnp.asarray(sizes, jnp.int32))

    sizes = jnp.where(number % 4 == 0, named(crowded, number // 4), named(usual, number - number // 4 - 1))
    mixed = jax.random.permutation(jax.random.fold_in(own, 3), count)
    donor, sink = mixed[0:count // 2 * 2:2], mixed[1:count // 2 * 2:2]
    room = jnp.minimum(sizes[donor] - 1, reach - sizes[sink]) // 2
    room = jnp.where((donor == sequence[0]) | (sink == sequence[0]) | (sizes[sink] == 0), 0, jnp.maximum(room, 0))
    shifted = jax.random.randint(jax.random.fold_in(own, 4), (count // 2,), 0, 1 << 20) % (room + 1)
    sizes = sizes.at[donor].add(-shifted).at[sink].add(shifted)
    labels = jnp.searchsorted(jnp.cumsum(sizes), jnp.arange(rows * top), side="right").astype(jnp.int32)
    table = labels.reshape(top, rows).T
    table = table[jax.random.permutation(jax.random.fold_in(own, 1), rows)]
    offset_by = jax.random.randint(jax.random.fold_in(own, 2), (rows, 1), 0, top)
    return jnp.take_along_axis(table, (jnp.arange(top)[None, :] + offset_by) % top, axis=1)


def load_shares(count, total, most, slope, full):
    portions = [(1 << 20) // math.isqrt(standing ** slope) + 1 for standing in range(1, count + 1)]
    largest = most if full else min(most, max(-(-total // count), total * portions[0] // sum(portions)))
    least = 1 if total - largest >= count - 1 else 0
    holding, surplus = [largest] + [least] * (count - 1), total - largest - least * (count - 1)
    while surplus > 0:
        movable = [i for i in range(1, count) if holding[i] < largest] or [i for i in range(1, count) if holding[i] < most]
        pool, remaining = sum([portions[i] for i in movable]), surplus
        for i in movable:
            extra = min(most - holding[i], max(1, remaining * portions[i] // pool), surplus)
            holding[i] = holding[i] + extra
            surplus = surplus - extra
    return np.array(holding)


def centred(rng, dims, spread, bound, pieces=(), kind=jnp.bfloat16):
    array = spread * jax.random.normal(rng, dims, jnp.float32)
    if pieces:
        array = array * block_levels(rng, dims, pieces, -0.22, 0.18)
    return jnp.clip(array, -bound, bound).astype(kind)


def setup_inputs(seed: int = 0) -> dict:
    streams_of = jax.random.split(jax.random.key(seed), 15)
    queries = draw_queries(jax.random.fold_in(streams_of[14], 71), 0)
    latent_cache = draw_latent_cache(jax.random.fold_in(streams_of[14], 71), 0)
    fresh_latent = centred(streams_of[2], (REQS, STEPS, LATENT), 1.0, 4.0, ((0, 32),))
    lengths = ragged_sizes(streams_of[3], REQS, REQS * LEN // 2, LEN, 2).astype(jnp.int32)
    handoff = set_ends((jax.random.randint(streams_of[4], (N_FFN, REQ_DEV), 0, 2) < 1).astype(jnp.int32), jax.random.fold_in(streams_of[4], 1), 0, 1)
    residual = draw_residual(jax.random.fold_in(streams_of[14], 71), 0)
    value_up_matrix = centred(streams_of[6], (HEADS, KV_RANK, V_HEAD), (KV_RANK // 4) ** -0.5, 0.5, ((0, 8),))
    output_weight = centred(streams_of[7], (HEADS * V_HEAD, D), (HEADS * V_HEAD // 8) ** -0.5, 0.1875, ((0, 8),))
    norm_gain = jnp.clip(jnp.exp(jax.random.uniform(streams_of[8], (D,), jnp.float32, math.log(0.3), math.log(3.0))), 0.3, 3.0)
    router = centred(streams_of[9], (D, EXPERTS), D ** -0.5, 0.0625)
    expert_ids_keys = jax.random.split(jax.random.fold_in(streams_of[10], 1), REQS * STEPS // (ROW_REQ * STEPS))
    expert_ids_turns = jax.random.permutation(jax.random.fold_in(streams_of[10], 3), REQS * STEPS // (ROW_REQ * STEPS))
    expert_ids = jax.vmap(lambda own, number: routed_block(jax.random.fold_in(streams_of[10], 2), own, number, ROW_REQ * STEPS, EXPERTS, TOP, CAP, 2))(expert_ids_keys, expert_ids_turns).reshape((REQS, STEPS, TOP))
    gate_weight = centred(streams_of[11], (EXPERTS, D, EXP_W), D ** -0.5, 0.0625, ((0, 8), (2, 4)))
    up_weight = centred(streams_of[12], (EXPERTS, D, EXP_W), D ** -0.5, 0.0625, ((0, 8), (2, 4)))
    down_weight = centred(streams_of[13], (EXPERTS, EXP_W, D), EXP_W ** -0.5, 0.125, ((0, 8), (1, 4)))
    return dict(queries=queries, latent_cache=latent_cache, fresh_latent=fresh_latent, lengths=lengths, handoff=handoff, residual=residual, value_up_matrix=value_up_matrix, output_weight=output_weight, norm_gain=norm_gain, router=router, expert_ids=expert_ids, gate_weight=gate_weight, up_weight=up_weight, down_weight=down_weight)


score_scale = 192.0 ** (-0.5)
norm_epsilon = 1e-06

def attend_one(item):
    queries, latent_cache, fresh_latent, sequence_length = item
    rows_flat = queries.reshape(STEPS * HEADS, LATENT)
    old_scores = jnp.dot(rows_flat, latent_cache.T, preferred_element_type=jnp.float32) * score_scale
    position = jnp.arange(LEN, dtype=jnp.int32)
    old_scores = jnp.where(position[None, :] < sequence_length, old_scores, -jnp.inf)
    new_scores = jnp.dot(rows_flat, fresh_latent.T, preferred_element_type=jnp.float32) * score_scale
    row_step = jnp.arange(STEPS * HEADS, dtype=jnp.int32) // HEADS
    column_step = jnp.arange(STEPS, dtype=jnp.int32)
    new_scores = jnp.where(column_step[None, :] <= row_step[:, None], new_scores, -jnp.inf)
    row_peak = jnp.maximum(lax.optimization_barrier(jnp.max(old_scores, axis=1)), lax.optimization_barrier(jnp.max(new_scores, axis=1)))[:, None]
    old_exp = jnp.exp(old_scores - row_peak)
    new_exp = jnp.exp(new_scores - row_peak)
    denominator = lax.optimization_barrier(jnp.sum(old_exp, axis=1, keepdims=True)) + lax.optimization_barrier(jnp.sum(new_exp, axis=1, keepdims=True))
    old_probs = (old_exp / denominator).astype(jnp.bfloat16)
    new_probs = (new_exp / denominator).astype(jnp.bfloat16)
    latent_mix = jnp.dot(old_probs, latent_cache[:, :KV_RANK], preferred_element_type=jnp.float32)
    latent_mix = latent_mix + jnp.dot(new_probs, fresh_latent[:, :KV_RANK], preferred_element_type=jnp.float32)
    return latent_mix.astype(jnp.bfloat16).reshape(STEPS, HEADS, KV_RANK)

def reference(queries, latent_cache, fresh_latent, lengths, handoff, residual, value_up_matrix, output_weight, norm_gain, router, expert_ids, gate_weight, up_weight, down_weight):
    latent_out = lax.map(attend_one, (queries, latent_cache, fresh_latent, lengths))
    grid = latent_out.reshape(N_ATTN, N_FFN, REQ_DEV, STEPS, HEADS, KV_RANK)
    rolled = jnp.roll(grid, 1, axis=0)
    placed_tokens = jnp.where(handoff[None, :, :, None, None, None] == 1, rolled, grid)
    placed_tokens = placed_tokens.reshape(REQS, STEPS, HEADS, KV_RANK)
    value_rows = jnp.einsum('olfb,fbw->olfw', placed_tokens.astype(jnp.float32), value_up_matrix.astype(jnp.float32)).astype(jnp.bfloat16)
    token_total = REQS * STEPS
    heads_out = jnp.dot(value_rows.reshape(token_total, HEADS * V_HEAD), output_weight, preferred_element_type=jnp.float32)
    state = residual.reshape(token_total, D).astype(jnp.float32) + heads_out
    attended = state.astype(jnp.bfloat16)
    scale_rows = lax.rsqrt(lax.optimization_barrier(jnp.mean(state * state, axis=1, keepdims=True)) + norm_epsilon)
    normed = (state * scale_rows * norm_gain.astype(jnp.float32)[None, :]).astype(jnp.bfloat16)
    logits = jnp.dot(normed, router, preferred_element_type=jnp.float32)
    affinity = jax.nn.sigmoid(logits)
    ids_flat = expert_ids.reshape(token_total, TOP)
    onehot = ids_flat[:, :, None] == jnp.arange(EXPERTS, dtype=jnp.int32)[None, None, :]
    chosen = lax.optimization_barrier(jnp.sum(jnp.where(onehot, affinity[:, None, :], jnp.float32(0.0)), axis=2))
    gate_fraction_value = 2.5 * chosen / lax.optimization_barrier(jnp.sum(chosen, axis=1, keepdims=True))
    weight_table = lax.optimization_barrier(jnp.sum(jnp.where(onehot, gate_fraction_value[:, :, None], jnp.float32(0.0)), axis=1))
    hit_table = lax.optimization_barrier(jnp.sum(onehot.astype(jnp.int32), axis=1))
    row_tokens = ROW_REQ * STEPS
    normed_blocks = normed.reshape(N_ATTN, row_tokens, D).astype(jnp.float32)
    slot_ids = jnp.arange(CAP, dtype=jnp.int32)

    def one_expert(carry, item):
        expert_index, gate_here, up_here, down_here = item
        token_hit = lax.optimization_barrier(jnp.sum(jnp.where(jnp.arange(EXPERTS, dtype=jnp.int32)[None, :] == expert_index, hit_table, 0), axis=1))
        token_weight = lax.optimization_barrier(jnp.sum(jnp.where(jnp.arange(EXPERTS, dtype=jnp.int32)[None, :] == expert_index, weight_table, jnp.float32(0.0)), axis=1))
        hit_blocks = token_hit.reshape(N_ATTN, row_tokens)
        slot_rank = jnp.cumsum(hit_blocks, axis=1) - 1
        selector = ((hit_blocks[:, None, :] == 1) & (slot_rank[:, None, :] == slot_ids[None, :, None])).astype(jnp.float32)
        expert_input = jnp.einsum('act,atd->acd', selector, normed_blocks).astype(jnp.bfloat16).reshape(N_ATTN * CAP, D)
        gate_part = jnp.dot(expert_input, gate_here, preferred_element_type=jnp.float32)
        up_part = jnp.dot(expert_input, up_here, preferred_element_type=jnp.float32)
        hidden_activations = (jax.nn.silu(gate_part) * up_part).astype(jnp.bfloat16)
        expert_rows = jnp.dot(hidden_activations, down_here, preferred_element_type=jnp.float32).astype(jnp.bfloat16)
        returned = jnp.einsum('act,acd->atd', selector, expert_rows.astype(jnp.float32).reshape(N_ATTN, CAP, D))
        return (carry + returned.reshape(token_total, D) * token_weight[:, None], None)
    initial = jnp.zeros((token_total, D), jnp.float32)
    combined, _ = lax.scan(one_expert, initial, (jnp.arange(EXPERTS, dtype=jnp.int32), gate_weight, up_weight, down_weight))
    expert_out = combined.astype(jnp.bfloat16).reshape(REQS, STEPS, D)
    return (attended.reshape(REQS, STEPS, D), expert_out)
```

```python
import functools

import jax
import jax.numpy as jnp
from jax import lax
from jax.experimental import pallas as pl
from jax.experimental.pallas import tpu as pltpu
from jax.sharding import PartitionSpec as P

KV_RANK = 512
SCORE_SCALE = 192.0 ** (-0.5)
NORM_EPSILON = 1e-06
IN_CHUNKS = 2
OUT_CHUNKS = 2

f32 = jnp.float32
bf16 = jnp.bfloat16


def swap(value, axis, mask):
    count = lax.axis_size(axis)
    return lax.ppermute(value, axis, [(i, i ^ mask) for i in range(count)])


def masks_of(count):
    return [1 << k for k in range(count.bit_length() - 1)]


def relative_order(count):
    order = [0]
    for mask in reversed(masks_of(count)):
        order = order + [mask ^ o for o in order]
    return order


def gather_rows(rows, axis):
    for mask in reversed(masks_of(lax.axis_size(axis))):
        rows = jnp.concatenate([rows, swap(rows, axis, mask)], axis=0)
    return rows


def reduce_rows(rows, axis, masks):
    for mask in masks:
        half = rows.shape[0] // 2
        rows = rows[:half] + swap(rows[half:].astype(bf16), axis, mask).astype(f32)
    return rows


def attend_kernel(heads_local, lengths_ref, q_ref, cache_ref, fresh_ref, out_ref):
    q = q_ref[0]
    row_count = q.shape[0]
    span = cache_ref.shape[1]
    steps = fresh_ref.shape[1]
    heads = row_count // steps
    live = lengths_ref[pl.program_id(0)]
    keys = cache_ref[0]
    contract = (((1,), (1,)), ((), ()))
    old = lax.dot_general(q, keys, contract, preferred_element_type=f32) * SCORE_SCALE
    position = lax.broadcasted_iota(jnp.int32, (row_count, span), 1)
    old = jnp.where(position < live, old, -jnp.inf)
    fresh = fresh_ref[0]
    new = lax.dot_general(q, fresh, contract, preferred_element_type=f32) * SCORE_SCALE
    row_step = lax.broadcasted_iota(jnp.int32, (row_count, steps), 0) // heads
    column = lax.broadcasted_iota(jnp.int32, (row_count, steps), 1)
    new = jnp.where(column <= row_step, new, -jnp.inf)
    peak = jnp.maximum(jnp.max(old, axis=1, keepdims=True), jnp.max(new, axis=1, keepdims=True))
    old_exp = jnp.exp(old - peak)
    new_exp = jnp.exp(new - peak)
    total = jnp.sum(old_exp, axis=1, keepdims=True) + jnp.sum(new_exp, axis=1, keepdims=True)
    inverse = 1.0 / total
    old_probs = (old_exp * inverse).astype(bf16)
    new_probs = (new_exp * inverse).astype(bf16).astype(f32)
    mix = jnp.dot(old_probs, keys[:, :KV_RANK], preferred_element_type=f32)
    fresh_values = fresh[:, :KV_RANK].astype(f32)
    for j in range(steps):
        mix = mix + new_probs[:, j : j + 1] * fresh_values[j : j + 1, :]
    if heads_local % 8 == 0:
        for dest in range(heads // heads_local):
            parts = [mix[t * heads + dest * heads_local :][:heads_local] for t in range(steps)]
            out_ref[dest, 0] = jnp.concatenate(parts, axis=0).astype(bf16)
    else:
        out_ref[0] = mix.astype(bf16)


def attend(queries, latent_cache, fresh_latent, lengths, heads_local):
    reqs, steps, heads, width = queries.shape
    span = latent_cache.shape[1]
    rows = steps * heads
    dests = heads // heads_local
    if heads_local % 8 == 0:
        out_shape = (dests, reqs, steps * heads_local, KV_RANK)
        out_spec = pl.BlockSpec(
            (dests, 1, steps * heads_local, KV_RANK), lambda r, n: (0, r, 0, 0)
        )
    else:
        out_shape = (reqs, rows, KV_RANK)
        out_spec = pl.BlockSpec((1, rows, KV_RANK), lambda r, n: (r, 0, 0))
    out = pl.pallas_call(
        functools.partial(attend_kernel, heads_local),
        out_shape=jax.ShapeDtypeStruct(out_shape, bf16),
        grid_spec=pltpu.PrefetchScalarGridSpec(
            num_scalar_prefetch=1,
            grid=(reqs,),
            in_specs=[
                pl.BlockSpec((1, rows, width), lambda r, n: (r, 0, 0)),
                pl.BlockSpec((1, span, width), lambda r, n: (r, 0, 0)),
                pl.BlockSpec((1, steps, width), lambda r, n: (r, 0, 0)),
            ],
            out_specs=out_spec,
        ),
        compiler_params=pltpu.CompilerParams(vmem_limit_bytes=24 * 1024 * 1024),
        name="attend",
    )(lengths, queries.reshape(reqs, rows, width), latent_cache, fresh_latent)
    if heads_local % 8 == 0:
        return out
    out = out.reshape(reqs, steps, dests, heads_local, KV_RANK)
    return out.transpose(2, 0, 1, 3, 4).reshape(dests, reqs, steps * heads_local, KV_RANK)


def value_kernel(order, place_ref, latent_ref, up_ref, out_ref):
    heads_local, _, v_head = up_ref.shape
    place = place_ref[0]
    rows = jnp.concatenate([latent_ref[place ^ o] for o in order], axis=0)
    tokens = rows.shape[0] // heads_local
    for h in range(heads_local):
        one = jnp.dot(rows, up_ref[h], preferred_element_type=f32)
        one = one.reshape(tokens, heads_local, v_head)
        head = lax.broadcasted_iota(jnp.int32, one.shape, 1)
        one = jnp.sum(jnp.where(head == h, one, 0.0), axis=1)
        out_ref[:, h * v_head : (h + 1) * v_head] = one.astype(bf16)


def values_of(latents, value_up, place, order):
    sources, reqs, rows, rank = latents.shape
    heads_local, _, v_head = value_up.shape
    steps = rows // heads_local
    tokens = sources * reqs * steps
    if heads_local % 8 == 0:
        return pl.pallas_call(
            functools.partial(value_kernel, order),
            out_shape=jax.ShapeDtypeStruct((tokens, heads_local * v_head), bf16),
            in_specs=[
                pl.BlockSpec(memory_space=pltpu.SMEM),
                pl.BlockSpec(memory_space=pltpu.VMEM),
                pl.BlockSpec(memory_space=pltpu.VMEM),
            ],
            out_specs=pl.BlockSpec(memory_space=pltpu.VMEM),
            compiler_params=pltpu.CompilerParams(vmem_limit_bytes=24 * 1024 * 1024),
            name="values",
        )(place[None], latents.reshape(sources, reqs * rows, rank), value_up)
    latents = latents[place ^ jnp.array(order, jnp.int32)]
    latents = latents.reshape(sources * reqs * steps, heads_local, rank)
    out = jnp.einsum("nhb,hbw->nhw", latents, value_up, preferred_element_type=f32)
    return out.astype(bf16).reshape(tokens, heads_local * v_head)


def local(
    queries,
    latent_cache,
    fresh_latent,
    lengths,
    handoff,
    residual,
    value_up_matrix,
    output_weight,
    norm_gain,
    router,
    expert_ids,
    gate_weight,
    up_weight,
    down_weight,
):
    n_attn = lax.axis_size("attn")
    n_ffn = lax.axis_size("ffn")
    attn_masks = masks_of(n_attn)
    ffn_masks = masks_of(n_ffn)
    order = relative_order(n_ffn)
    ffn_index = lax.axis_index("ffn").astype(jnp.int32)
    sources = ffn_index ^ jnp.array(order, jnp.int32)
    reqs, steps, model_width = residual.shape
    own_tokens = reqs * steps
    row_tokens = n_ffn * own_tokens
    heads_local = value_up_matrix.shape[0]

    ids = expert_ids.reshape(n_ffn, own_tokens, expert_ids.shape[2])[sources]
    ids = ids.reshape(row_tokens, expert_ids.shape[2])
    hit = jnp.sum((ids == ffn_index).astype(jnp.int32), axis=1)
    rank = jnp.cumsum(hit) - 1
    capacity = 4 * own_tokens
    slots = lax.broadcasted_iota(jnp.int32, (capacity, row_tokens), 0)
    chosen = (hit[None, :] == 1) & (rank[None, :] == slots)
    selector = chosen.astype(bf16)
    partner_id = jnp.sum(
        jnp.where(chosen, (jnp.sum(ids, axis=1) - ffn_index)[None, :], 0), axis=1
    )
    moved = lax.all_gather(handoff[0], "ffn", axis=0)[sources]
    moved = jnp.repeat(moved.reshape(n_ffn * reqs) == 1, steps)[:, None]

    latents = attend(queries, latent_cache, fresh_latent, lengths, heads_local)
    latents = lax.all_to_all(latents, "ffn", split_axis=0, concat_axis=0, tiled=True)
    values = values_of(latents, value_up_matrix, ffn_index, order)
    arrived = lax.ppermute(values, "attn", [(i, (i + 1) % n_attn) for i in range(n_attn)])
    values = jnp.where(moved, arrived, values)

    residual_rows = residual.reshape(own_tokens, model_width)
    half_tokens = row_tokens // 2
    width = model_width // IN_CHUNKS
    attended = []
    selected = []
    for c in range(IN_CHUNKS):
        columns = slice(c * width, (c + 1) * width)
        weight = output_weight[:, columns]
        outgoing = jnp.dot(values[half_tokens:], weight, preferred_element_type=f32).astype(bf16)
        incoming = swap(outgoing, "ffn", ffn_masks[0])
        part = jnp.dot(values[:half_tokens], weight, preferred_element_type=f32)
        part = reduce_rows(part + incoming.astype(f32), "ffn", ffn_masks[1:])
        state = residual_rows[:, columns].astype(f32) + part
        attended.append(state.astype(bf16))
        gained = (state * norm_gain[None, columns]).astype(bf16)
        gained = gather_rows(gained, "ffn")
        rows = jnp.dot(selector, gained, preferred_element_type=f32).astype(bf16)
        selected.append(gather_rows(rows, "attn"))
    attended = jnp.concatenate(attended, axis=1).reshape(reqs, steps, model_width)

    gate_part = up_part = squares = logits = 0.0
    for c in range(IN_CHUNKS):
        columns = slice(c * width, (c + 1) * width)
        rows = selected[c]
        gate_part += jnp.dot(rows, gate_weight[0, columns], preferred_element_type=f32)
        up_part += jnp.dot(rows, up_weight[0, columns], preferred_element_type=f32)
        inverse_gain = 1.0 / norm_gain[None, columns]
        squares += jnp.sum(jnp.square(rows.astype(f32) * inverse_gain), axis=1, keepdims=True)
        logits += jnp.dot(rows[:capacity], router[columns], preferred_element_type=f32)
    scale = lax.rsqrt(squares / model_width + NORM_EPSILON)
    hidden = (jax.nn.silu(gate_part * scale) * (up_part * scale)).astype(bf16)
    affinity = jax.nn.sigmoid(logits * scale[:capacity])
    expert = lax.broadcasted_iota(jnp.int32, affinity.shape, 1)
    mine = jnp.sum(jnp.where(expert == ffn_index, affinity, 0.0), axis=1, keepdims=True)
    other = jnp.sum(jnp.where(expert == partner_id[:, None], affinity, 0.0), axis=1, keepdims=True)
    share = 2.5 * mine / (mine + other)

    half_rows = hidden.shape[0] // 2
    width = model_width // OUT_CHUNKS
    spread = (((0,), (0,)), ((), ()))
    result = []
    for c in range(OUT_CHUNKS):
        columns = slice(c * width, (c + 1) * width)
        weight = down_weight[0][:, columns]
        outgoing = jnp.dot(hidden[half_rows:], weight, preferred_element_type=f32).astype(bf16)
        incoming = swap(outgoing, "attn", attn_masks[0])
        part = jnp.dot(hidden[:half_rows], weight, preferred_element_type=f32)
        part = reduce_rows(part + incoming.astype(f32), "attn", attn_masks[1:])
        rows = (part * share).astype(bf16)
        outgoing = lax.dot_general(
            selector[:, half_tokens:], rows, spread, preferred_element_type=f32
        ).astype(bf16)
        incoming = swap(outgoing, "ffn", ffn_masks[0])
        part = lax.dot_general(
            selector[:, :half_tokens], rows, spread, preferred_element_type=f32
        )
        part = reduce_rows(part + incoming.astype(f32), "ffn", ffn_masks[1:])
        result.append(part.astype(bf16))
    result = jnp.concatenate(result, axis=1).reshape(reqs, steps, model_width)
    return attended, result


def solution(mesh):
    return jax.shard_map(
        local,
        mesh=mesh,
        in_specs=(
            P(("attn", "ffn"), None, None, None),
            P(("attn", "ffn"), None, None),
            P(("attn", "ffn"), None, None),
            P(("attn", "ffn")),
            P("ffn", None),
            P(("attn", "ffn"), None, None),
            P("ffn", None, None),
            P("ffn", None),
            P(),
            P(),
            P("attn", None, None),
            P("ffn", None, "attn"),
            P("ffn", None, "attn"),
            P("ffn", "attn", None),
        ),
        out_specs=(P(("attn", "ffn"), None, None), P(("attn", "ffn"), None, None)),
        check_vma=False,
    )
```

```python
import functools
import math

import jax
import jax.numpy as jnp
from jax import lax
from jax.experimental import pallas as pl
from jax.experimental.pallas import tpu as pltpu
from jax.sharding import PartitionSpec as P

KV_RANK = 512
SCORE_SCALE = 192.0 ** (-0.5)
NORM_EPSILON = 1e-06
MIB = 1024 * 1024
STATE_WIDTHS = (28, 28)
IN_WIDTHS = (14, 14, 14, 14)
OUT_WIDTHS = (14, 14, 14, 14)
PROJECT_TILE = 896
PROJECT_SPLITS = 4

f32 = jnp.float32
bf16 = jnp.bfloat16


def swap(value, axis, mask):
    count = lax.axis_size(axis)
    return lax.ppermute(value, axis, [(i, i ^ mask) for i in range(count)])


def column_ranges(shares, model_width):
    unit = model_width // sum(shares)
    return [(sum(shares[:i]) * unit, share * unit) for i, share in enumerate(shares)]


def masks_of(count):
    return [1 << k for k in range(count.bit_length() - 1)]


def relative_order(count):
    order = [0]
    for mask in reversed(masks_of(count)):
        order = order + [mask ^ o for o in order]
    return order


def gather_rows(rows, axis):
    for mask in reversed(masks_of(lax.axis_size(axis))):
        rows = jnp.concatenate([rows, swap(rows, axis, mask)], axis=0)
    return rows


def reduce_rows(rows, axis, masks):
    for mask in masks:
        half = rows.shape[0] // 2
        rows = rows[:half] + swap(rows[half:].astype(bf16), axis, mask).astype(f32)
    return rows


def in_hbm(array):
    return pltpu.with_memory_space_constraint(array, pltpu.HBM)


def attend_request(q, keys, fresh, live):
    row_count = q.shape[0]
    span = keys.shape[1]
    steps = fresh.shape[0]
    heads = row_count // steps
    old = jnp.dot(q, keys, preferred_element_type=f32) * SCORE_SCALE
    position = lax.broadcasted_iota(jnp.int32, (row_count, span), 1)
    old = jnp.where(position < live, old, -jnp.inf)
    step = lax.broadcasted_iota(jnp.int32, (row_count, 1), 0) // heads
    fresh = fresh.astype(f32)
    wide = q.astype(f32)
    peak = jnp.max(old, axis=1, keepdims=True)
    new = []
    for j in range(steps):
        score = jnp.sum(wide * fresh[j : j + 1], axis=1, keepdims=True) * SCORE_SCALE
        new.append(jnp.where(step >= j, score, -jnp.inf))
        peak = jnp.maximum(peak, new[j])
    old = jnp.exp(old - peak)
    new = [jnp.exp(score - peak) for score in new]
    total = jnp.sum(old, axis=1, keepdims=True)
    contract = (((1,), (1,)), ((), ()))
    mix = lax.dot_general(old.astype(bf16), keys[:KV_RANK], contract, preferred_element_type=f32)
    for j in range(steps):
        total = total + new[j]
        mix = mix + new[j] * fresh[j : j + 1, :KV_RANK]
    return mix * (1.0 / total)


def attend_kernel(masks, heads_local, lengths_ref, place_ref, q_ref, cache_ref, fresh_ref, *refs):
    outs, mix_ref = refs[:-1], refs[-1]
    count, steps = q_ref.shape[0], fresh_ref.shape[1]
    heads = q_ref.shape[1] // steps
    place = place_ref[0]
    base = pl.program_id(0) * count
    for r in range(count):
        mix_ref[r] = attend_request(q_ref[r], cache_ref[r], fresh_ref[r], lengths_ref[base + r])
        if masks is None:
            outs[0][r] = mix_ref[r].astype(bf16)
            continue
        for out_ref, pair in zip(outs, masks):
            for far, mask in enumerate(pair):
                first = (place ^ mask) * heads_local
                parts = [
                    mix_ref[r, pl.ds(pl.multiple_of(t * heads + first, 8), heads_local)]
                    for t in range(steps)
                ]
                out_ref[far, r] = jnp.concatenate(parts, axis=0).astype(bf16)


def attend(queries, latent_cache, fresh_latent, lengths, place, masks, heads_local):
    reqs, steps, heads, width = queries.shape
    span = latent_cache.shape[1]
    rows = steps * heads
    group = 4 if reqs % 4 == 0 else 1
    if masks is not None:
        rows_local = steps * heads_local
        out_shape = [
            jax.ShapeDtypeStruct((len(pair), reqs, rows_local, KV_RANK), bf16) for pair in masks
        ]
        out_specs = [
            pl.BlockSpec((len(pair), group, rows_local, KV_RANK), lambda r, n, p: (0, r, 0, 0))
            for pair in masks
        ]
    else:
        out_shape = [jax.ShapeDtypeStruct((reqs, rows, KV_RANK), bf16)]
        out_specs = [pl.BlockSpec((group, rows, KV_RANK), lambda r, n, p: (r, 0, 0))]
    return pl.pallas_call(
        functools.partial(attend_kernel, masks, heads_local),
        out_shape=out_shape,
        grid_spec=pltpu.PrefetchScalarGridSpec(
            num_scalar_prefetch=2,
            grid=(reqs // group,),
            in_specs=[
                pl.BlockSpec((group, rows, width), lambda r, n, p: (r, 0, 0)),
                pl.BlockSpec((group, width, span), lambda r, n, p: (r, 0, 0)),
                pl.BlockSpec((group, steps, width), lambda r, n, p: (r, 0, 0)),
            ],
            out_specs=out_specs,
            scratch_shapes=[pltpu.VMEM((group, rows, KV_RANK), f32)],
        ),
        compiler_params=pltpu.CompilerParams(vmem_limit_bytes=24 * MIB),
        cost_estimate=pl.CostEstimate(
            flops=4 * reqs * rows * span * width,
            bytes_accessed=2 * reqs * span * width,
            transcendentals=reqs * rows * span,
        ),
        name="attend",
    )(
        lengths,
        place[None],
        in_hbm(queries.reshape(reqs, rows, width)),
        in_hbm(latent_cache.transpose(0, 2, 1)),
        fresh_latent,
    )


def value_kernel(far, order, place_ref, *refs):
    latent_refs, up_ref, out_ref = refs[:-2], refs[-2], refs[-1]
    heads_local, _, v_head = up_ref.shape
    share = heads_local // len(order)
    place = place_ref[0]
    rows = jnp.concatenate([latent_ref[far] for latent_ref in latent_refs], axis=0)
    tokens = rows.shape[0] // heads_local
    for i in range(heads_local):
        own = (place ^ order[i // share]) * share + i % share if len(order) > 1 else i
        one = jnp.dot(rows, up_ref[i], preferred_element_type=f32)
        one = one.reshape(tokens, heads_local, v_head)
        head = lax.broadcasted_iota(jnp.int32, one.shape, 1)
        one = jnp.sum(jnp.where(head == own, one, 0.0), axis=1)
        first = own * v_head
        if len(order) > 1:
            first = pl.multiple_of(first, 128)
        out_ref[:, pl.ds(first, v_head)] = one.astype(bf16)


def values_of(latents, far, value_up, place, order):
    heads_local, _, v_head = value_up.shape
    pairs, reqs, rows, rank = latents[0].shape
    tokens = len(latents) * reqs * rows // heads_local
    whole = pl.BlockSpec(memory_space=pltpu.VMEM)
    return pl.pallas_call(
        functools.partial(value_kernel, far, order),
        out_shape=jax.ShapeDtypeStruct((tokens, heads_local * v_head), bf16),
        in_specs=[pl.BlockSpec(memory_space=pltpu.SMEM)] + [whole] * (len(latents) + 1),
        out_specs=whole,
        compiler_params=pltpu.CompilerParams(vmem_limit_bytes=12 * MIB),
        cost_estimate=pl.CostEstimate(
            flops=2 * tokens * heads_local * heads_local * rank * v_head,
            bytes_accessed=2 * value_up.size,
            transcendentals=0,
        ),
        name="values",
    )(place[None], *[x.reshape(pairs, reqs * rows, rank) for x in latents], value_up)


def values_here(queries, latent_cache, fresh_latent, lengths, value_up):
    n_attn, n_ffn = lax.axis_size("attn"), lax.axis_size("ffn")
    attn_index = lax.axis_index("attn").astype(jnp.int32)
    ffn_index = lax.axis_index("ffn").astype(jnp.int32)
    far = n_ffn // 2
    near = relative_order(far)
    heads_local, rank, v_head = value_up.shape
    reqs, steps = queries.shape[:2]
    if heads_local % 8 == 0 and heads_local % n_attn == 0:
        share = heads_local // n_attn
        part = lax.dynamic_slice_in_dim(value_up, attn_index * share, share, 0)
        partner_up = gather_rows(swap(part, "ffn", far), "attn")
        masks = [(m, m ^ far) for m in near]
        latents = attend(
            queries, latent_cache, fresh_latent, lengths, ffn_index, masks, heads_local
        )
        latents = [x if m == 0 else swap(x, "ffn", m) for x, m in zip(latents, near)]
        partner = values_of(latents, 1, partner_up, attn_index, relative_order(n_attn))
        arrived = swap(partner, "ffn", far)
        latents[0], _ = lax.optimization_barrier((latents[0], partner))
        return values_of(latents, 0, value_up, attn_index, [0]), arrived
    (latents,) = attend(queries, latent_cache, fresh_latent, lengths, ffn_index, None, heads_local)
    latents = latents.reshape(reqs, steps, n_ffn, heads_local, rank)
    latents = lax.all_to_all(latents, "ffn", split_axis=2, concat_axis=0, tiled=True)
    latents = latents.reshape(n_ffn, reqs * steps, heads_local, rank)
    values = []
    for flip in (0, far):
        rows = latents[ffn_index ^ jnp.array([m ^ flip for m in near], jnp.int32)]
        rows = rows.reshape(-1, heads_local, rank)
        rows = jnp.einsum("nhb,hbw->nhw", rows, value_up, preferred_element_type=f32)
        values.append(rows.astype(bf16).reshape(-1, heads_local * v_head))
    return values


def project_kernel(values_ref, *refs):
    weight_refs, (kept_ref, sent_ref) = refs[:-2], refs[-2:]
    half = kept_ref.shape[0]
    depth = weight_refs[0].shape[0]
    out = 0.0
    for i, weight_ref in enumerate(weight_refs):
        rows = values_ref[:, i * depth : (i + 1) * depth]
        out = out + jnp.dot(rows, weight_ref[...], preferred_element_type=f32)
    kept_ref[...] = out[:half]
    sent_ref[...] = out[half:].astype(bf16)


def project(values, weight, first, width):
    tokens, depth = values.shape
    tile = math.gcd(math.gcd(first, width), PROJECT_TILE)
    half = tokens // 2
    offset = first // tile
    splits = PROJECT_SPLITS
    weight_specs = [
        pl.BlockSpec((depth // splits, tile), lambda j, i=i: (i, offset + j)) for i in range(splits)
    ]
    return pl.pallas_call(
        project_kernel,
        out_shape=(
            jax.ShapeDtypeStruct((half, width), f32),
            jax.ShapeDtypeStruct((half, width), bf16),
        ),
        grid=(width // tile,),
        in_specs=[pl.BlockSpec((tokens, depth), lambda j: (0, 0)), *weight_specs],
        out_specs=(
            pl.BlockSpec((half, tile), lambda j: (0, j)),
            pl.BlockSpec((half, tile), lambda j: (0, j)),
        ),
        compiler_params=pltpu.CompilerParams(vmem_limit_bytes=12 * MIB),
        cost_estimate=pl.CostEstimate(
            flops=2 * tokens * depth * width, bytes_accessed=2 * depth * width, transcendentals=0
        ),
        name="project",
    )(values, *[in_hbm(weight)] * splits)


def local(
    queries,
    latent_cache,
    fresh_latent,
    lengths,
    handoff,
    residual,
    value_up_matrix,
    output_weight,
    norm_gain,
    router,
    expert_ids,
    gate_weight,
    up_weight,
    down_weight,
):
    n_attn = lax.axis_size("attn")
    n_ffn = lax.axis_size("ffn")
    attn_masks = masks_of(n_attn)
    ffn_masks = masks_of(n_ffn)
    order = relative_order(n_ffn)
    ffn_index = lax.axis_index("ffn").astype(jnp.int32)
    sources = ffn_index ^ jnp.array(order, jnp.int32)
    reqs, steps, model_width = residual.shape
    own_tokens = reqs * steps
    row_tokens = n_ffn * own_tokens
    heads_local = value_up_matrix.shape[0]

    ids = expert_ids.reshape(n_ffn, own_tokens, expert_ids.shape[2])[sources]
    ids = ids.reshape(row_tokens, expert_ids.shape[2])
    hit = jnp.sum((ids == ffn_index).astype(jnp.int32), axis=1)
    rank = jnp.cumsum(hit) - 1
    capacity = 4 * own_tokens
    slots = lax.broadcasted_iota(jnp.int32, (capacity, row_tokens), 0)
    chosen = (hit[None, :] == 1) & (rank[None, :] == slots)
    selector = chosen.astype(bf16)
    partner_id = jnp.sum(
        jnp.where(chosen, (jnp.sum(ids, axis=1) - ffn_index)[None, :], 0), axis=1
    )

    residual_rows = residual.reshape(own_tokens, model_width)
    half_tokens = row_tokens // 2
    moved = jnp.repeat(handoff[0] == 1, steps)[:, None]
    onward = [(i, (i + 1) % n_attn) for i in range(n_attn)]
    near_values, far_values = values_here(
        queries, latent_cache, fresh_latent, lengths, value_up_matrix
    )

    def near_sum(values, first, width):
        part, outgoing = project(values, output_weight, first, width)
        part = part + swap(outgoing, "ffn", ffn_masks[0]).astype(f32)
        return reduce_rows(part, "ffn", ffn_masks[1:-1])

    state_ranges = column_ranges(STATE_WIDTHS, model_width)
    near_sums = [near_sum(near_values, *columns) for columns in state_ranges]
    sums = []
    for part, columns in zip(near_sums, state_ranges):
        outgoing = near_sum(far_values, *columns).astype(bf16)
        part = part + swap(outgoing, "ffn", ffn_masks[-1]).astype(f32)
        arrived = lax.ppermute(part.astype(bf16), "attn", onward).astype(f32)
        sums.append(jnp.where(moved, arrived, part))

    def total_of(first, width):
        pieces = []
        for (start, wide), piece in zip(state_ranges, sums):
            low, high = max(first, start), min(first + width, start + wide)
            if low < high:
                pieces.append(piece[:, low - start : high - start])
        return pieces[0] if len(pieces) == 1 else jnp.concatenate(pieces, axis=1)

    attended = []
    selected = []
    for first, width in column_ranges(IN_WIDTHS, model_width):
        columns = slice(first, first + width)
        state = residual_rows[:, columns].astype(f32) + total_of(first, width)
        attended.append(state.astype(bf16))
        gained = (state * norm_gain[None, columns]).astype(bf16)
        gained = gather_rows(gained, "ffn")
        rows = jnp.dot(selector, gained, preferred_element_type=f32).astype(bf16)
        selected.append(gather_rows(rows, "attn"))
    attended = jnp.concatenate(attended, axis=1).reshape(reqs, steps, model_width)

    gate_part = up_part = squares = logits = 0.0
    for rows, (first, width) in zip(selected, column_ranges(IN_WIDTHS, model_width)):
        columns = slice(first, first + width)
        gate_part += jnp.dot(rows, gate_weight[0, columns], preferred_element_type=f32)
        up_part += jnp.dot(rows, up_weight[0, columns], preferred_element_type=f32)
        inverse_gain = 1.0 / norm_gain[None, columns]
        squares += jnp.sum(jnp.square(rows.astype(f32) * inverse_gain), axis=1, keepdims=True)
        logits += jnp.dot(rows[:capacity], router[columns], preferred_element_type=f32)
    scale = lax.rsqrt(squares / model_width + NORM_EPSILON)
    hidden = (jax.nn.silu(gate_part * scale) * (up_part * scale)).astype(bf16)
    affinity = jax.nn.sigmoid(logits * scale[:capacity])
    expert = lax.broadcasted_iota(jnp.int32, affinity.shape, 1)
    mine = jnp.sum(jnp.where(expert == ffn_index, affinity, 0.0), axis=1, keepdims=True)
    other = jnp.sum(jnp.where(expert == partner_id[:, None], affinity, 0.0), axis=1, keepdims=True)
    share = 2.5 * mine / (mine + other)
    weights = jnp.sum(jnp.where(chosen, share, 0.0), axis=0)[:, None]

    half_rows = hidden.shape[0] // 2
    spread = (((0,), (0,)), ((), ()))
    result = []
    for first, width in column_ranges(OUT_WIDTHS, model_width):
        weight = down_weight[0][:, first : first + width]
        outgoing = jnp.dot(hidden[half_rows:], weight, preferred_element_type=f32).astype(bf16)
        incoming = swap(outgoing, "attn", attn_masks[0])
        part = jnp.dot(hidden[:half_rows], weight, preferred_element_type=f32)
        part = reduce_rows(part + incoming.astype(f32), "attn", attn_masks[1:])
        rows = part.astype(bf16)
        outgoing = lax.dot_general(
            selector[:, half_tokens:], rows, spread, preferred_element_type=f32
        )
        outgoing = (outgoing * weights[half_tokens:]).astype(bf16)
        incoming = swap(outgoing, "ffn", ffn_masks[0])
        part = lax.dot_general(
            selector[:, :half_tokens], rows, spread, preferred_element_type=f32
        )
        part = part * weights[:half_tokens]
        part = reduce_rows(part + incoming.astype(f32), "ffn", ffn_masks[1:])
        result.append(part.astype(bf16))
    result = jnp.concatenate(result, axis=1).reshape(reqs, steps, model_width)
    return attended, result


def solution(mesh):
    return jax.shard_map(
        local,
        mesh=mesh,
        in_specs=(
            P(("attn", "ffn"), None, None, None),
            P(("attn", "ffn"), None, None),
            P(("attn", "ffn"), None, None),
            P(("attn", "ffn")),
            P("ffn", None),
            P(("attn", "ffn"), None, None),
            P("ffn", None, None),
            P("ffn", None),
            P(),
            P(),
            P("attn", None, None),
            P("ffn", None, "attn"),
            P("ffn", None, "attn"),
            P("ffn", "attn", None),
        ),
        out_specs=(P(("attn", "ffn"), None, None), P(("attn", "ffn"), None, None)),
        check_vma=False,
    )
```

```python
import functools
import math

import jax
import jax.numpy as jnp
from jax import lax
from jax.experimental import pallas as pl
from jax.experimental.pallas import tpu as pltpu
from jax.sharding import PartitionSpec as P

KV_RANK = 512
SCORE_SCALE = 192.0 ** (-0.5)
NORM_EPSILON = 1e-06
MIB = 1024 * 1024
STATE_WIDTHS = (28, 28)
IN_WIDTHS = (14, 14, 14, 14)
OUT_WIDTHS = (14, 14, 14, 14)
PROJECT_TILE = 1792
PROJECT_SPLITS = 4

f32 = jnp.float32
bf16 = jnp.bfloat16


def swap(value, axis, mask):
    count = lax.axis_size(axis)
    return lax.ppermute(value, axis, [(i, i ^ mask) for i in range(count)])


def column_ranges(shares, model_width):
    unit = model_width // sum(shares)
    return [(sum(shares[:i]) * unit, share * unit) for i, share in enumerate(shares)]


def masks_of(count):
    return [1 << k for k in range(count.bit_length() - 1)]


def relative_order(count):
    order = [0]
    for mask in reversed(masks_of(count)):
        order = order + [mask ^ o for o in order]
    return order


def gather_rows(rows, axis, masks=None):
    for mask in reversed(masks or masks_of(lax.axis_size(axis))):
        rows = jnp.concatenate([rows, swap(rows, axis, mask)], axis=0)
    return rows


def reduce_rows(rows, axis, masks):
    for mask in masks:
        half = rows.shape[0] // 2
        rows = rows[:half] + swap(rows[half:].astype(bf16), axis, mask).astype(f32)
    return rows


def in_hbm(array):
    return pltpu.with_memory_space_constraint(array, pltpu.HBM)


def attend_request(q, keys, fresh, live):
    row_count = q.shape[0]
    span = keys.shape[1]
    steps = fresh.shape[0]
    heads = row_count // steps
    old = jnp.dot(q, keys, preferred_element_type=f32) * SCORE_SCALE
    position = lax.broadcasted_iota(jnp.int32, (row_count, span), 1)
    old = jnp.where(position < live, old, -jnp.inf)
    step = lax.broadcasted_iota(jnp.int32, (row_count, 1), 0) // heads
    fresh = fresh.astype(f32)
    wide = q.astype(f32)
    peak = jnp.max(old, axis=1, keepdims=True)
    new = []
    for j in range(steps):
        score = jnp.sum(wide * fresh[j : j + 1], axis=1, keepdims=True) * SCORE_SCALE
        new.append(jnp.where(step >= j, score, -jnp.inf))
        peak = jnp.maximum(peak, new[j])
    old = jnp.exp(old - peak)
    new = [jnp.exp(score - peak) for score in new]
    total = jnp.sum(old, axis=1, keepdims=True)
    contract = (((1,), (1,)), ((), ()))
    mix = lax.dot_general(old.astype(bf16), keys[:KV_RANK], contract, preferred_element_type=f32)
    for j in range(steps):
        total = total + new[j]
        mix = mix + new[j] * fresh[j : j + 1, :KV_RANK]
    return mix * (1.0 / total)


def attend_kernel(masks, heads_local, lengths_ref, place_ref, q_ref, cache_ref, fresh_ref, *refs):
    outs, mix_ref = refs[:-1], refs[-1]
    count, steps = q_ref.shape[0], fresh_ref.shape[1]
    heads = q_ref.shape[1] // steps
    place = place_ref[0]
    base = pl.program_id(0) * count
    for r in range(count):
        mix_ref[r] = attend_request(q_ref[r], cache_ref[r], fresh_ref[r], lengths_ref[base + r])
        if masks is None:
            outs[0][r] = mix_ref[r].astype(bf16)
            continue
        for out_ref, pair in zip(outs, masks):
            for far, mask in enumerate(pair):
                first = (place ^ mask) * heads_local
                parts = [
                    mix_ref[r, pl.ds(pl.multiple_of(t * heads + first, 8), heads_local)]
                    for t in range(steps)
                ]
                out_ref[far, r] = jnp.concatenate(parts, axis=0).astype(bf16)


def attend(queries, latent_cache, fresh_latent, lengths, place, masks, heads_local):
    reqs, steps, heads, width = queries.shape
    span = latent_cache.shape[1]
    rows = steps * heads
    group = 4 if reqs % 4 == 0 else 1
    if masks is not None:
        rows_local = steps * heads_local
        out_shape = [
            jax.ShapeDtypeStruct((len(pair), reqs, rows_local, KV_RANK), bf16) for pair in masks
        ]
        out_specs = [
            pl.BlockSpec((len(pair), group, rows_local, KV_RANK), lambda r, n, p: (0, r, 0, 0))
            for pair in masks
        ]
    else:
        out_shape = [jax.ShapeDtypeStruct((reqs, rows, KV_RANK), bf16)]
        out_specs = [pl.BlockSpec((group, rows, KV_RANK), lambda r, n, p: (r, 0, 0))]
    return pl.pallas_call(
        functools.partial(attend_kernel, masks, heads_local),
        out_shape=out_shape,
        grid_spec=pltpu.PrefetchScalarGridSpec(
            num_scalar_prefetch=2,
            grid=(reqs // group,),
            in_specs=[
                pl.BlockSpec((group, rows, width), lambda r, n, p: (r, 0, 0)),
                pl.BlockSpec((group, width, span), lambda r, n, p: (r, 0, 0)),
                pl.BlockSpec((group, steps, width), lambda r, n, p: (r, 0, 0)),
            ],
            out_specs=out_specs,
            scratch_shapes=[pltpu.VMEM((group, rows, KV_RANK), f32)],
        ),
        compiler_params=pltpu.CompilerParams(vmem_limit_bytes=24 * MIB),
        cost_estimate=pl.CostEstimate(
            flops=4 * reqs * rows * span * width,
            bytes_accessed=2 * reqs * span * width,
            transcendentals=reqs * rows * span,
        ),
        name="attend",
    )(
        lengths,
        place[None],
        in_hbm(queries.reshape(reqs, rows, width)),
        in_hbm(latent_cache.transpose(0, 2, 1)),
        in_hbm(fresh_latent),
    )


def value_kernel(far, order, place_ref, *refs):
    latent_refs, up_ref, out_ref = refs[:-2], refs[-2], refs[-1]
    heads_local, _, v_head = up_ref.shape
    share = heads_local // len(order)
    place = place_ref[0]
    rows = jnp.concatenate([latent_ref[far] for latent_ref in latent_refs], axis=0)
    tokens = rows.shape[0] // heads_local
    for i in range(heads_local):
        own = (place ^ order[i // share]) * share + i % share if len(order) > 1 else i
        one = jnp.dot(rows, up_ref[i], preferred_element_type=f32)
        one = one.reshape(tokens, heads_local, v_head)
        head = lax.broadcasted_iota(jnp.int32, one.shape, 1)
        one = jnp.sum(jnp.where(head == own, one, 0.0), axis=1)
        first = own * v_head
        if len(order) > 1:
            first = pl.multiple_of(first, 128)
        out_ref[:, pl.ds(first, v_head)] = one.astype(bf16)


def values_of(latents, far, value_up, place, order):
    heads_local, _, v_head = value_up.shape
    pairs, reqs, rows, rank = latents[0].shape
    tokens = len(latents) * reqs * rows // heads_local
    whole = pl.BlockSpec(memory_space=pltpu.VMEM)
    return pl.pallas_call(
        functools.partial(value_kernel, far, order),
        out_shape=jax.ShapeDtypeStruct((tokens, heads_local * v_head), bf16),
        in_specs=[pl.BlockSpec(memory_space=pltpu.SMEM)] + [whole] * (len(latents) + 1),
        out_specs=whole,
        compiler_params=pltpu.CompilerParams(vmem_limit_bytes=12 * MIB),
        cost_estimate=pl.CostEstimate(
            flops=2 * tokens * heads_local * heads_local * rank * v_head,
            bytes_accessed=2 * value_up.size,
            transcendentals=0,
        ),
        name="values",
    )(place[None], *[x.reshape(pairs, reqs * rows, rank) for x in latents], value_up)


def values_here(queries, latent_cache, fresh_latent, lengths, handoff, value_up):
    n_attn, n_ffn = lax.axis_size("attn"), lax.axis_size("ffn")
    attn_index = lax.axis_index("attn").astype(jnp.int32)
    ffn_index = lax.axis_index("ffn").astype(jnp.int32)
    far = n_ffn // 2
    near = relative_order(far)
    heads_local, rank, v_head = value_up.shape
    reqs, steps = queries.shape[:2]
    onward = [(i, (i + 1) % n_attn) for i in range(n_attn)]

    def hand_off(values, moved):
        return jnp.where(moved, lax.ppermute(values, "attn", onward), values)

    if heads_local % 8 == 0 and heads_local % n_attn == 0:
        share = heads_local // n_attn
        part = lax.dynamic_slice_in_dim(value_up, attn_index * share, share, 0)
        partner_up = gather_rows(swap(part, "ffn", far), "attn")
        masks = [(m, m ^ far) for m in near]
        latents = attend(
            queries, latent_cache, fresh_latent, lengths, ffn_index, masks, heads_local
        )
        latents = [x if m == 0 else swap(x, "ffn", m) for x, m in zip(latents, near)]
        moved = gather_rows(handoff, "ffn", masks_of(far))
        moved = jnp.repeat(moved.reshape(-1) == 1, steps)[:, None]
        partner = values_of(latents, 1, partner_up, attn_index, relative_order(n_attn))
        latents[0], _ = lax.optimization_barrier((latents[0], partner))
        arrived = swap(hand_off(partner, moved), "ffn", far)
        return hand_off(values_of(latents, 0, value_up, attn_index, [0]), moved), arrived
    (latents,) = attend(queries, latent_cache, fresh_latent, lengths, ffn_index, None, heads_local)
    latents = latents.reshape(reqs, steps, n_ffn, heads_local, rank)
    latents = lax.all_to_all(latents, "ffn", split_axis=2, concat_axis=0, tiled=True)
    latents = latents.reshape(n_ffn, reqs * steps, heads_local, rank)
    flags = lax.all_gather(handoff[0], "ffn", axis=0)
    values = []
    for flip in (0, far):
        sources = ffn_index ^ jnp.array([m ^ flip for m in near], jnp.int32)
        moved = jnp.repeat(flags[sources].reshape(-1) == 1, steps)[:, None]
        rows = latents[sources]
        rows = rows.reshape(-1, heads_local, rank)
        rows = jnp.einsum("nhb,hbw->nhw", rows, value_up, preferred_element_type=f32)
        values.append(hand_off(rows.astype(bf16).reshape(-1, heads_local * v_head), moved))
    return values


def project_kernel(first, values_ref, weight_ref, kept_ref, sent_ref, held, sems):
    tiles, depth, tile = held.shape
    splits = sems.shape[1]
    rows = depth // splits
    half = kept_ref.shape[0]
    copies = []
    for i in range(tiles):
        columns = pl.ds(first + i * tile, tile)
        for s in range(splits):
            block = pl.ds(s * rows, rows)
            copies.append(
                pltpu.make_async_copy(
                    weight_ref.at[block, columns], held.at[i, block], sems.at[i, s]
                )
            )
    for copy in copies:
        copy.start()
    values = values_ref[...]
    for i in range(tiles):
        for copy in copies[i * splits : (i + 1) * splits]:
            copy.wait()
        out = jnp.dot(values, held[i], preferred_element_type=f32)
        columns = pl.ds(i * tile, tile)
        kept_ref[:, columns] = out[:half]
        sent_ref[:, columns] = out[half:].astype(bf16)


def project(values, weight, first, width):
    tokens, depth = values.shape
    tile = math.gcd(width, PROJECT_TILE)
    half = tokens // 2
    tiles = width // tile
    return pl.pallas_call(
        functools.partial(project_kernel, first),
        out_shape=(
            jax.ShapeDtypeStruct((half, width), f32),
            jax.ShapeDtypeStruct((half, width), bf16),
        ),
        in_specs=[
            pl.BlockSpec((tokens, depth), lambda: (0, 0)),
            pl.BlockSpec(memory_space=pl.ANY),
        ],
        out_specs=(
            pl.BlockSpec((half, width), lambda: (0, 0)),
            pl.BlockSpec((half, width), lambda: (0, 0)),
        ),
        scratch_shapes=[
            pltpu.VMEM((tiles, depth, tile), bf16),
            pltpu.SemaphoreType.DMA((tiles, PROJECT_SPLITS)),
        ],
        compiler_params=pltpu.CompilerParams(vmem_limit_bytes=16 * MIB),
        cost_estimate=pl.CostEstimate(
            flops=2 * tokens * depth * width, bytes_accessed=2 * depth * width, transcendentals=0
        ),
        name="project",
    )(values, in_hbm(weight))


def local(
    queries,
    latent_cache,
    fresh_latent,
    lengths,
    handoff,
    residual,
    value_up_matrix,
    output_weight,
    norm_gain,
    router,
    expert_ids,
    gate_weight,
    up_weight,
    down_weight,
):
    n_attn = lax.axis_size("attn")
    n_ffn = lax.axis_size("ffn")
    attn_masks = masks_of(n_attn)
    ffn_masks = masks_of(n_ffn)
    order = relative_order(n_ffn)
    ffn_index = lax.axis_index("ffn").astype(jnp.int32)
    sources = ffn_index ^ jnp.array(order, jnp.int32)
    reqs, steps, model_width = residual.shape
    own_tokens = reqs * steps
    row_tokens = n_ffn * own_tokens
    heads_local = value_up_matrix.shape[0]

    ids = expert_ids.reshape(n_ffn, own_tokens, expert_ids.shape[2])[sources]
    ids = ids.reshape(row_tokens, expert_ids.shape[2])
    hit = jnp.sum((ids == ffn_index).astype(jnp.int32), axis=1)
    rank = jnp.cumsum(hit) - 1
    capacity = 4 * own_tokens
    slots = lax.broadcasted_iota(jnp.int32, (capacity, row_tokens), 0)
    chosen = (hit[None, :] == 1) & (rank[None, :] == slots)
    selector = chosen.astype(bf16)
    partner_id = jnp.sum(
        jnp.where(chosen, (jnp.sum(ids, axis=1) - ffn_index)[None, :], 0), axis=1
    )

    residual_rows = residual.reshape(own_tokens, model_width)
    half_tokens = row_tokens // 2
    near_values, far_values = values_here(
        queries, latent_cache, fresh_latent, lengths, handoff, value_up_matrix
    )

    def near_sum(values, first, width):
        part, outgoing = project(values, output_weight, first, width)
        part = part + swap(outgoing, "ffn", ffn_masks[0]).astype(f32)
        return reduce_rows(part, "ffn", ffn_masks[1:-1])

    state_ranges = column_ranges(STATE_WIDTHS, model_width)
    near_sums = [near_sum(near_values, *columns) for columns in state_ranges]
    sums = []
    for part, columns in zip(near_sums, state_ranges):
        outgoing = near_sum(far_values, *columns).astype(bf16)
        sums.append(part + swap(outgoing, "ffn", ffn_masks[-1]).astype(f32))

    def total_of(first, width):
        pieces = []
        for (start, wide), piece in zip(state_ranges, sums):
            low, high = max(first, start), min(first + width, start + wide)
            if low < high:
                pieces.append(piece[:, low - start : high - start])
        return pieces[0] if len(pieces) == 1 else jnp.concatenate(pieces, axis=1)

    attended = []
    selected = []
    for first, width in column_ranges(IN_WIDTHS, model_width):
        columns = slice(first, first + width)
        state = residual_rows[:, columns].astype(f32) + total_of(first, width)
        attended.append(state.astype(bf16))
        gained = (state * norm_gain[None, columns]).astype(bf16)
        gained = gather_rows(gained, "ffn")
        rows = jnp.dot(selector, gained, preferred_element_type=f32).astype(bf16)
        selected.append(gather_rows(rows, "attn"))
    attended = jnp.concatenate(attended, axis=1).reshape(reqs, steps, model_width)

    gate_part = up_part = squares = logits = 0.0
    for rows, (first, width) in zip(selected, column_ranges(IN_WIDTHS, model_width)):
        columns = slice(first, first + width)
        gate_part += jnp.dot(rows, gate_weight[0, columns], preferred_element_type=f32)
        up_part += jnp.dot(rows, up_weight[0, columns], preferred_element_type=f32)
        inverse_gain = 1.0 / norm_gain[None, columns]
        squares += jnp.sum(jnp.square(rows.astype(f32) * inverse_gain), axis=1, keepdims=True)
        logits += jnp.dot(rows[:capacity], router[columns], preferred_element_type=f32)
    scale = lax.rsqrt(squares / model_width + NORM_EPSILON)
    hidden = (jax.nn.silu(gate_part * scale) * (up_part * scale)).astype(bf16)
    affinity = jax.nn.sigmoid(logits * scale[:capacity])
    expert = lax.broadcasted_iota(jnp.int32, affinity.shape, 1)
    mine = jnp.sum(jnp.where(expert == ffn_index, affinity, 0.0), axis=1, keepdims=True)
    other = jnp.sum(jnp.where(expert == partner_id[:, None], affinity, 0.0), axis=1, keepdims=True)
    share = 2.5 * mine / (mine + other)
    weights = jnp.sum(jnp.where(chosen, share, 0.0), axis=0)[:, None]

    half_rows = hidden.shape[0] // 2
    spread = (((0,), (0,)), ((), ()))
    result = []
    for first, width in column_ranges(OUT_WIDTHS, model_width):
        weight = down_weight[0][:, first : first + width]
        outgoing = jnp.dot(hidden[half_rows:], weight, preferred_element_type=f32).astype(bf16)
        incoming = swap(outgoing, "attn", attn_masks[0])
        part = jnp.dot(hidden[:half_rows], weight, preferred_element_type=f32)
        part = reduce_rows(part + incoming.astype(f32), "attn", attn_masks[1:])
        rows = part.astype(bf16)
        outgoing = lax.dot_general(
            selector[:, half_tokens:], rows, spread, preferred_element_type=f32
        )
        outgoing = (outgoing * weights[half_tokens:]).astype(bf16)
        incoming = swap(outgoing, "ffn", ffn_masks[0])
        part = lax.dot_general(
            selector[:, :half_tokens], rows, spread, preferred_element_type=f32
        )
        part = part * weights[:half_tokens]
        part = reduce_rows(part + incoming.astype(f32), "ffn", ffn_masks[1:])
        result.append(part.astype(bf16))
    result = jnp.concatenate(result, axis=1).reshape(reqs, steps, model_width)
    return attended, result


def solution(mesh):
    return jax.shard_map(
        local,
        mesh=mesh,
        in_specs=(
            P(("attn", "ffn"), None, None, None),
            P(("attn", "ffn"), None, None),
            P(("attn", "ffn"), None, None),
            P(("attn", "ffn")),
            P("ffn", None),
            P(("attn", "ffn"), None, None),
            P("ffn", None, None),
            P("ffn", None),
            P(),
            P(),
            P("attn", None, None),
            P("ffn", None, "attn"),
            P("ffn", None, "attn"),
            P("ffn", "attn", None),
        ),
        out_specs=(P(("attn", "ffn"), None, None), P(("attn", "ffn"), None, None)),
        check_vma=False,
    )
```

```python
import functools
import math

import jax
import jax.numpy as jnp
from jax import lax
from jax.experimental import pallas as pl
from jax.experimental.pallas import tpu as pltpu
from jax.sharding import PartitionSpec as P

KV_RANK = 512
SCORE_SCALE = 192.0 ** (-0.5)
NORM_EPSILON = 1e-06
MIB = 1024 * 1024
STATE_WIDTHS = (28, 28)
IN_WIDTHS = (14, 14, 14, 14)
OUT_WIDTHS = (14, 14, 14, 14)
PROJECT_TILE = 1792
PROJECT_SPLITS = 8

f32 = jnp.float32
bf16 = jnp.bfloat16


def swap(value, axis, mask):
    count = lax.axis_size(axis)
    return lax.ppermute(value, axis, [(i, i ^ mask) for i in range(count)])


def column_ranges(shares, model_width):
    unit = model_width // sum(shares)
    return [(sum(shares[:i]) * unit, share * unit) for i, share in enumerate(shares)]


def masks_of(count):
    return [1 << k for k in range(count.bit_length() - 1)]


def relative_order(count):
    order = [0]
    for mask in reversed(masks_of(count)):
        order = order + [mask ^ o for o in order]
    return order


def gather_rows(rows, axis, masks=None):
    for mask in reversed(masks or masks_of(lax.axis_size(axis))):
        rows = jnp.concatenate([rows, swap(rows, axis, mask)], axis=0)
    return rows


def reduce_rows(rows, axis, masks):
    for mask in masks:
        half = rows.shape[0] // 2
        rows = rows[:half] + swap(rows[half:].astype(bf16), axis, mask).astype(f32)
    return rows


def in_hbm(array):
    return pltpu.with_memory_space_constraint(array, pltpu.HBM)


def attend_request(q, keys, fresh, live):
    row_count = q.shape[0]
    span = keys.shape[1]
    steps = fresh.shape[0]
    heads = row_count // steps
    old = jnp.dot(q, keys, preferred_element_type=f32) * SCORE_SCALE
    position = lax.broadcasted_iota(jnp.int32, (row_count, span), 1)
    old = jnp.where(position < live, old, -jnp.inf)
    step = lax.broadcasted_iota(jnp.int32, (row_count, 1), 0) // heads
    fresh = fresh.astype(f32)
    wide = q.astype(f32)
    peak = jnp.max(old, axis=1, keepdims=True)
    new = []
    for j in range(steps):
        score = jnp.sum(wide * fresh[j : j + 1], axis=1, keepdims=True) * SCORE_SCALE
        new.append(jnp.where(step >= j, score, -jnp.inf))
        peak = jnp.maximum(peak, new[j])
    old = jnp.exp(old - peak)
    new = [jnp.exp(score - peak) for score in new]
    total = jnp.sum(old, axis=1, keepdims=True)
    contract = (((1,), (1,)), ((), ()))
    mix = lax.dot_general(old.astype(bf16), keys[:KV_RANK], contract, preferred_element_type=f32)
    for j in range(steps):
        total = total + new[j]
        mix = mix + new[j] * fresh[j : j + 1, :KV_RANK]
    return mix * (1.0 / total)


def attend_kernel(masks, heads_local, lengths_ref, place_ref, q_ref, cache_ref, fresh_ref, *refs):
    outs, mix_ref = refs[:-1], refs[-1]
    count, steps = q_ref.shape[0], fresh_ref.shape[1]
    heads = q_ref.shape[1] // steps
    place = place_ref[0]
    base = pl.program_id(0) * count
    for r in range(count):
        mix_ref[r] = attend_request(q_ref[r], cache_ref[r], fresh_ref[r], lengths_ref[base + r])
        if masks is None:
            outs[0][r] = mix_ref[r].astype(bf16)
            continue
        for out_ref, pair in zip(outs, masks):
            for far, mask in enumerate(pair):
                first = (place ^ mask) * heads_local
                parts = [
                    mix_ref[r, pl.ds(pl.multiple_of(t * heads + first, 8), heads_local)]
                    for t in range(steps)
                ]
                out_ref[far, r] = jnp.concatenate(parts, axis=0).astype(bf16)


def attend(queries, latent_cache, fresh_latent, lengths, place, masks, heads_local):
    reqs, steps, heads, width = queries.shape
    span = latent_cache.shape[1]
    rows = steps * heads
    group = 4 if reqs % 4 == 0 else 1
    if masks is not None:
        rows_local = steps * heads_local
        out_shape = [
            jax.ShapeDtypeStruct((len(pair), reqs, rows_local, KV_RANK), bf16) for pair in masks
        ]
        out_specs = [
            pl.BlockSpec((len(pair), group, rows_local, KV_RANK), lambda r, n, p: (0, r, 0, 0))
            for pair in masks
        ]
    else:
        out_shape = [jax.ShapeDtypeStruct((reqs, rows, KV_RANK), bf16)]
        out_specs = [pl.BlockSpec((group, rows, KV_RANK), lambda r, n, p: (r, 0, 0))]
    return pl.pallas_call(
        functools.partial(attend_kernel, masks, heads_local),
        out_shape=out_shape,
        grid_spec=pltpu.PrefetchScalarGridSpec(
            num_scalar_prefetch=2,
            grid=(reqs // group,),
            in_specs=[
                pl.BlockSpec((group, rows, width), lambda r, n, p: (r, 0, 0)),
                pl.BlockSpec((group, width, span), lambda r, n, p: (r, 0, 0)),
                pl.BlockSpec((group, steps, width), lambda r, n, p: (r, 0, 0)),
            ],
            out_specs=out_specs,
            scratch_shapes=[pltpu.VMEM((group, rows, KV_RANK), f32)],
        ),
        compiler_params=pltpu.CompilerParams(vmem_limit_bytes=24 * MIB),
        cost_estimate=pl.CostEstimate(
            flops=4 * reqs * rows * span * width,
            bytes_accessed=2 * reqs * span * width,
            transcendentals=reqs * rows * span,
        ),
        name="attend",
    )(
        lengths,
        place[None],
        in_hbm(queries.reshape(reqs, rows, width)),
        in_hbm(latent_cache.transpose(0, 2, 1)),
        in_hbm(fresh_latent),
    )


def value_kernel(far, order, place_ref, *refs):
    latent_refs, up_ref, out_ref = refs[:-2], refs[-2], refs[-1]
    heads_local, _, v_head = up_ref.shape
    share = heads_local // len(order)
    place = place_ref[0]
    rows = jnp.concatenate([latent_ref[far] for latent_ref in latent_refs], axis=0)
    tokens = rows.shape[0] // heads_local
    for i in range(heads_local):
        own = (place ^ order[i // share]) * share + i % share if len(order) > 1 else i
        one = jnp.dot(rows, up_ref[i], preferred_element_type=f32)
        one = one.reshape(tokens, heads_local, v_head)
        head = lax.broadcasted_iota(jnp.int32, one.shape, 1)
        one = jnp.sum(jnp.where(head == own, one, 0.0), axis=1)
        first = own * v_head
        if len(order) > 1:
            first = pl.multiple_of(first, 128)
        out_ref[:, pl.ds(first, v_head)] = one.astype(bf16)


def values_of(latents, far, value_up, place, order):
    heads_local, _, v_head = value_up.shape
    pairs, reqs, rows, rank = latents[0].shape
    tokens = len(latents) * reqs * rows // heads_local
    whole = pl.BlockSpec(memory_space=pltpu.VMEM)
    return pl.pallas_call(
        functools.partial(value_kernel, far, order),
        out_shape=jax.ShapeDtypeStruct((tokens, heads_local * v_head), bf16),
        in_specs=[pl.BlockSpec(memory_space=pltpu.SMEM)] + [whole] * (len(latents) + 1),
        out_specs=whole,
        compiler_params=pltpu.CompilerParams(vmem_limit_bytes=12 * MIB),
        cost_estimate=pl.CostEstimate(
            flops=2 * tokens * heads_local * heads_local * rank * v_head,
            bytes_accessed=2 * value_up.size,
            transcendentals=0,
        ),
        name="values",
    )(place[None], *[x.reshape(pairs, reqs * rows, rank) for x in latents], value_up)


def values_here(queries, latent_cache, fresh_latent, lengths, handoff, value_up):
    n_attn, n_ffn = lax.axis_size("attn"), lax.axis_size("ffn")
    attn_index = lax.axis_index("attn").astype(jnp.int32)
    ffn_index = lax.axis_index("ffn").astype(jnp.int32)
    far = n_ffn // 2
    near = relative_order(far)
    heads_local, rank, v_head = value_up.shape
    reqs, steps = queries.shape[:2]
    onward = [(i, (i + 1) % n_attn) for i in range(n_attn)]

    def hand_off(values, moved):
        return jnp.where(moved, lax.ppermute(values, "attn", onward), values)

    if heads_local % 8 == 0 and heads_local % n_attn == 0:
        share = heads_local // n_attn
        part = lax.dynamic_slice_in_dim(value_up, attn_index * share, share, 0)
        partner_up = gather_rows(swap(part, "ffn", far), "attn")
        masks = [(m, m ^ far) for m in near]
        latents = attend(
            queries, latent_cache, fresh_latent, lengths, ffn_index, masks, heads_local
        )
        latents = [x if m == 0 else swap(x, "ffn", m) for x, m in zip(latents, near)]
        moved = gather_rows(handoff, "ffn", masks_of(far))
        moved = jnp.repeat(moved.reshape(-1) == 1, steps)[:, None]
        partner = values_of(latents, 1, partner_up, attn_index, relative_order(n_attn))
        latents[0], _ = lax.optimization_barrier((latents[0], partner))
        arrived = swap(hand_off(partner, moved), "ffn", far)
        return hand_off(values_of(latents, 0, value_up, attn_index, [0]), moved), arrived
    (latents,) = attend(queries, latent_cache, fresh_latent, lengths, ffn_index, None, heads_local)
    latents = latents.reshape(reqs, steps, n_ffn, heads_local, rank)
    latents = lax.all_to_all(latents, "ffn", split_axis=2, concat_axis=0, tiled=True)
    latents = latents.reshape(n_ffn, reqs * steps, heads_local, rank)
    flags = lax.all_gather(handoff[0], "ffn", axis=0)
    values = []
    for flip in (0, far):
        sources = ffn_index ^ jnp.array([m ^ flip for m in near], jnp.int32)
        moved = jnp.repeat(flags[sources].reshape(-1) == 1, steps)[:, None]
        rows = latents[sources]
        rows = rows.reshape(-1, heads_local, rank)
        rows = jnp.einsum("nhb,hbw->nhw", rows, value_up, preferred_element_type=f32)
        values.append(hand_off(rows.astype(bf16).reshape(-1, heads_local * v_head), moved))
    return values


def project_kernel(first, values_ref, weight_ref, kept_ref, sent_ref, held, sems):
    tiles, depth, tile = held.shape
    splits = sems.shape[1]
    rows = depth // splits
    half = kept_ref.shape[0]
    copies = []
    for i in range(tiles):
        columns = pl.ds(first + i * tile, tile)
        for s in range(splits):
            block = pl.ds(s * rows, rows)
            copies.append(
                pltpu.make_async_copy(
                    weight_ref.at[block, columns], held.at[i, block], sems.at[i, s]
                )
            )
    for copy in copies:
        copy.start()
    values = values_ref[...]
    for i in range(tiles):
        for copy in copies[i * splits : (i + 1) * splits]:
            copy.wait()
        out = jnp.dot(values, held[i], preferred_element_type=f32)
        columns = pl.ds(i * tile, tile)
        kept_ref[:, columns] = out[:half]
        sent_ref[:, columns] = out[half:].astype(bf16)


def project(values, weight, first, width):
    tokens, depth = values.shape
    tile = math.gcd(width, PROJECT_TILE)
    half = tokens // 2
    tiles = width // tile
    return pl.pallas_call(
        functools.partial(project_kernel, first),
        out_shape=(
            jax.ShapeDtypeStruct((half, width), f32),
            jax.ShapeDtypeStruct((half, width), bf16),
        ),
        in_specs=[
            pl.BlockSpec((tokens, depth), lambda: (0, 0)),
            pl.BlockSpec(memory_space=pl.ANY),
        ],
        out_specs=(
            pl.BlockSpec((half, width), lambda: (0, 0)),
            pl.BlockSpec((half, width), lambda: (0, 0)),
        ),
        scratch_shapes=[
            pltpu.VMEM((tiles, depth, tile), bf16),
            pltpu.SemaphoreType.DMA((tiles, PROJECT_SPLITS)),
        ],
        compiler_params=pltpu.CompilerParams(vmem_limit_bytes=16 * MIB),
        cost_estimate=pl.CostEstimate(
            flops=2 * tokens * depth * width, bytes_accessed=2 * depth * width, transcendentals=0
        ),
        name="project",
    )(values, in_hbm(weight))


def local(
    queries,
    latent_cache,
    fresh_latent,
    lengths,
    handoff,
    residual,
    value_up_matrix,
    output_weight,
    norm_gain,
    router,
    expert_ids,
    gate_weight,
    up_weight,
    down_weight,
):
    n_attn = lax.axis_size("attn")
    n_ffn = lax.axis_size("ffn")
    attn_masks = masks_of(n_attn)
    ffn_masks = masks_of(n_ffn)
    order = relative_order(n_ffn)
    ffn_index = lax.axis_index("ffn").astype(jnp.int32)
    sources = ffn_index ^ jnp.array(order, jnp.int32)
    reqs, steps, model_width = residual.shape
    own_tokens = reqs * steps
    row_tokens = n_ffn * own_tokens
    heads_local = value_up_matrix.shape[0]

    ids = expert_ids.reshape(n_ffn, own_tokens, expert_ids.shape[2])[sources]
    ids = ids.reshape(row_tokens, expert_ids.shape[2])
    hit = jnp.sum((ids == ffn_index).astype(jnp.int32), axis=1)
    rank = jnp.cumsum(hit) - 1
    capacity = 4 * own_tokens
    slots = lax.broadcasted_iota(jnp.int32, (capacity, row_tokens), 0)
    chosen = (hit[None, :] == 1) & (rank[None, :] == slots)
    selector = chosen.astype(bf16)
    partner_id = jnp.sum(
        jnp.where(chosen, (jnp.sum(ids, axis=1) - ffn_index)[None, :], 0), axis=1
    )

    residual_rows = residual.reshape(own_tokens, model_width)
    half_tokens = row_tokens // 2
    near_values, far_values = values_here(
        queries, latent_cache, fresh_latent, lengths, handoff, value_up_matrix
    )

    def near_sum(values, first, width):
        part, outgoing = project(values, output_weight, first, width)
        part = part + swap(outgoing, "ffn", ffn_masks[0]).astype(f32)
        return reduce_rows(part, "ffn", ffn_masks[1:-1])

    state_ranges = column_ranges(STATE_WIDTHS, model_width)
    near_sums = [near_sum(near_values, *columns) for columns in state_ranges]
    sums = []
    for part, columns in zip(near_sums, state_ranges):
        outgoing = near_sum(far_values, *columns).astype(bf16)
        sums.append(part + swap(outgoing, "ffn", ffn_masks[-1]).astype(f32))

    def total_of(first, width):
        pieces = []
        for (start, wide), piece in zip(state_ranges, sums):
            low, high = max(first, start), min(first + width, start + wide)
            if low < high:
                pieces.append(piece[:, low - start : high - start])
        return pieces[0] if len(pieces) == 1 else jnp.concatenate(pieces, axis=1)

    attended = []
    selected = []
    for first, width in column_ranges(IN_WIDTHS, model_width):
        columns = slice(first, first + width)
        state = residual_rows[:, columns].astype(f32) + total_of(first, width)
        attended.append(state.astype(bf16))
        gained = (state * norm_gain[None, columns]).astype(bf16)
        gained = gather_rows(gained, "ffn")
        rows = jnp.dot(selector, gained, preferred_element_type=f32).astype(bf16)
        selected.append(gather_rows(rows, "attn"))
    attended = jnp.concatenate(attended, axis=1).reshape(reqs, steps, model_width)

    gate_part = up_part = squares = logits = 0.0
    for rows, (first, width) in zip(selected, column_ranges(IN_WIDTHS, model_width)):
        columns = slice(first, first + width)
        gate_part += jnp.dot(rows, gate_weight[0, columns], preferred_element_type=f32)
        up_part += jnp.dot(rows, up_weight[0, columns], preferred_element_type=f32)
        inverse_gain = 1.0 / norm_gain[None, columns]
        squares += jnp.sum(jnp.square(rows.astype(f32) * inverse_gain), axis=1, keepdims=True)
        logits += jnp.dot(rows[:capacity], router[columns], preferred_element_type=f32)
    scale = lax.rsqrt(squares / model_width + NORM_EPSILON)
    hidden = (jax.nn.silu(gate_part * scale) * (up_part * scale)).astype(bf16)
    affinity = jax.nn.sigmoid(logits * scale[:capacity])
    expert = lax.broadcasted_iota(jnp.int32, affinity.shape, 1)
    mine = jnp.sum(jnp.where(expert == ffn_index, affinity, 0.0), axis=1, keepdims=True)
    other = jnp.sum(jnp.where(expert == partner_id[:, None], affinity, 0.0), axis=1, keepdims=True)
    share = 2.5 * mine / (mine + other)
    weights = jnp.sum(jnp.where(chosen, share, 0.0), axis=0)[:, None]

    half_rows = hidden.shape[0] // 2
    spread = (((0,), (0,)), ((), ()))
    result = []
    for first, width in column_ranges(OUT_WIDTHS, model_width):
        weight = down_weight[0][:, first : first + width]
        outgoing = jnp.dot(hidden[half_rows:], weight, preferred_element_type=f32).astype(bf16)
        incoming = swap(outgoing, "attn", attn_masks[0])
        part = jnp.dot(hidden[:half_rows], weight, preferred_element_type=f32)
        part = reduce_rows(part + incoming.astype(f32), "attn", attn_masks[1:])
        rows = part.astype(bf16)
        outgoing = lax.dot_general(
            selector[:, half_tokens:], rows, spread, preferred_element_type=f32
        )
        outgoing = (outgoing * weights[half_tokens:]).astype(bf16)
        incoming = swap(outgoing, "ffn", ffn_masks[0])
        part = lax.dot_general(
            selector[:, :half_tokens], rows, spread, preferred_element_type=f32
        )
        part = part * weights[:half_tokens]
        part = reduce_rows(part + incoming.astype(f32), "ffn", ffn_masks[1:])
        result.append(part.astype(bf16))
    result = jnp.concatenate(result, axis=1).reshape(reqs, steps, model_width)
    return attended, result


def solution(mesh):
    return jax.shard_map(
        local,
        mesh=mesh,
        in_specs=(
            P(("attn", "ffn"), None, None, None),
            P(("attn", "ffn"), None, None),
            P(("attn", "ffn"), None, None),
            P(("attn", "ffn")),
            P("ffn", None),
            P(("attn", "ffn"), None, None),
            P("ffn", None, None),
            P("ffn", None),
            P(),
            P(),
            P("attn", None, None),
            P("ffn", None, "attn"),
            P("ffn", None, "attn"),
            P("ffn", "attn", None),
        ),
        out_specs=(P(("attn", "ffn"), None, None), P(("attn", "ffn"), None, None)),
        check_vma=False,
    )
```
